32 devices in a mesh: feat: 4 (over x, core), rows: 8 (over z, y).
Axes of the slice: x: 2, y: 2, z: 4, core: 2. Of those that a mesh axis runs over, the one named last changes fastest.
Arguments:
- samples: float32 [440, 32768], P(None, ('feat', 'rows')), may hold values from -6 to 6, as said below
- residual: float32 [147, 32768], P(None, ('feat', 'rows')), may hold values from -12 to 12, as said below
- bank: float32 [8, 440, 1024], P(None, None, 'feat'), may hold values from -0.25 to 0.25
- bank_phase: float32 [8, 1024], P(None, 'feat'), may hold values from -3.140625 to 3.140625
- bank_weights: float32 [8, 147, 1024], P(None, None, 'feat'), may hold values from -4 to 4
- block_index: int32 [1], replicated, may hold values from 0 to 7
Outputs:
- new_weights: float32 [147, 1024], P(None, 'feat')
- new_residual: float32 [147, 32768], P(None, ('feat', 'rows'))
The draws below stay inside these ranges and needn't reach their ends.
Inputs may be any that keep to these rules, and one draw needn't show every extreme that they name: `samples`: frames of the input features. `residual`: targets that depend partly on the frames.
All inputs are finite; a program needn't handle non-finite values.
Results may differ from the reference program's by a relative error of at most 0.0003.
Values sent between devices are 32-bit elements; how exact they have to be, the bound alone decides.
A program may use at most 128 MiB of HBM per device.

```python
import jax
import jax.numpy as jnp
from jax import lax

D = 440
C = 147
FB = 1024
NBLK = 8
ROW_DEV = 1024
NTOT = 32768
N_ROWS = 8


def frames_from(key):
    inner = jax.random.fold_in(key, 7)
    values = jax.random.normal(inner, (D, NTOT), jnp.float32)
    return jnp.clip(values, -6.0, 6.0)


def draw_samples(key, part):
    return frames_from(key)


def draw_residual(key, part):
    frames = frames_from(key)
    mixing = jax.random.normal(jax.random.fold_in(key, 11), (C, D), jnp.float32) * D ** (-0.5)
    noise = jax.random.normal(jax.random.fold_in(key, 13), (C, NTOT), jnp.float32)
    values = jnp.dot(mixing, frames) + 0.5 * noise
    return jnp.clip(values, -12.0, 12.0)


def shard_levels(key, shape, split, smallest, high):
    def one(dim, parts):
        heights = jax.random.uniform(jax.random.fold_in(jax.random.fold_in(key, 6), dim), (parts,), jnp.float32, smallest / len(split), high / len(split))
        return jnp.repeat(jnp.exp(heights), shape[dim] // parts).reshape((-1,) + (1,) * (len(shape) - dim - 1))

    level = one(*split[0])
    for cut in split[1:]:
        level = level * one(*cut)
    return level


def scatter_about(stream_key, dims, scale, most, cuts=(), kind=jnp.bfloat16):
    array = jax.random.normal(stream_key, dims, jnp.float32) * scale
    if len(cuts) > 0:
        array = shard_levels(stream_key, dims, cuts, -0.22, 0.18) * array
    return jnp.clip(array, min=-most, max=most).astype(kind)


def setup_inputs(seed: int = 0) -> dict:
    keys = jax.random.split(jax.random.key(seed), 7)
    samples = draw_samples(jax.random.fold_in(keys[6], 71), 0)
    residual = draw_residual(jax.random.fold_in(keys[6], 71), 0)
    bank = scatter_about(keys[2], (NBLK, D, FB), D ** -0.5, 0.25, ((2, 4),), jnp.float32)
    bank_phase = jnp.clip(jax.random.uniform(keys[3], (NBLK, FB), jnp.float32, -3.140625, 3.140625), -3.140625, 3.140625)
    bank_weights = scatter_about(keys[4], (NBLK, C, FB), 0.5, 4.0, ((2, 4),), jnp.float32)
    block_index = jax.random.randint(keys[5], (1,), 0, NBLK).astype(jnp.int32)
    return {"samples": samples, "residual": residual, "bank": bank, "bank_phase": bank_phase, "bank_weights": bank_weights, "block_index": block_index}


ridge_weight = 0.05

def features_of(projection, phases, block):
    inner = lax.dot_general(projection.astype(jnp.float32), block.astype(jnp.float32), (((0,), (0,)), ((), ())), precision=lax.Precision.HIGHEST, preferred_element_type=jnp.float32)
    return jnp.cos(inner + phases[:, None])

def reference(samples, residual, bank, bank_phase, bank_weights, block_index):
    chosen = block_index[0]
    projection = lax.dynamic_index_in_dim(bank, chosen, 0, keepdims=False)
    phases = lax.dynamic_index_in_dim(bank_phase, chosen, 0, keepdims=False)
    weights = lax.dynamic_index_in_dim(bank_weights, chosen, 0, keepdims=False)
    width = ROW_DEV * N_ROWS
    count = NTOT // width

    def accumulate(index, carry):
        gram, right = carry
        start = (index * width).astype(jnp.int32)
        block = lax.dynamic_slice_in_dim(samples, start, width, 1)
        target = lax.dynamic_slice_in_dim(residual, start, width, 1)
        features = features_of(projection, phases, block)
        gram = gram + lax.dot_general(features.astype(jnp.float32), features.astype(jnp.float32), (((1,), (1,)), ((), ())), precision=lax.Precision.HIGHEST, preferred_element_type=jnp.float32)
        right = right + lax.dot_general(features.astype(jnp.float32), target.astype(jnp.float32), (((1,), (1,)), ((), ())), precision=lax.Precision.HIGHEST, preferred_element_type=jnp.float32)
        return (gram, right)
    start_carry = (jnp.zeros((FB, FB), jnp.float32), jnp.zeros((FB, C), jnp.float32))
    gram, right = lax.fori_loop(0, count, accumulate, start_carry)
    system = gram / NTOT + ridge_weight * jnp.eye(FB, dtype=jnp.float32)
    right = right / NTOT - ridge_weight * weights.T
    factor = jnp.linalg.cholesky(system)
    middle = lax.linalg.triangular_solve(factor, right, left_side=True, lower=True)
    update_block = lax.linalg.triangular_solve(factor, middle, left_side=True, lower=True, transpose_a=True)
    new_weights = weights + update_block.T

    def correct(index, current):
        start = (index * width).astype(jnp.int32)
        block = lax.dynamic_slice_in_dim(samples, start, width, 1)
        target = lax.dynamic_slice_in_dim(current, start, width, 1)
        features = features_of(projection, phases, block)
        fitted = lax.dot_general(update_block.astype(jnp.float32), features.astype(jnp.float32), (((0,), (0,)), ((), ())), precision=lax.Precision.HIGHEST, preferred_element_type=jnp.float32)
        return lax.dynamic_update_slice_in_dim(current, target - fitted, start, 1)
    new_residual = lax.fori_loop(0, count, correct, residual)
    return (new_weights, new_residual)
```

```python
import functools
import math

import jax
import jax.numpy as jnp
from jax import lax
from jax.experimental import pallas as pl
from jax.experimental.pallas import tpu as pltpu
from jax.sharding import PartitionSpec as P

ridge_weight = 0.05
WIDE = 256
PANEL = 128
SUB = 8
SINE = (3.141592640144165, -5.167710084047848, 2.550077528428822, -0.598291299770303, 0.07765766117753167)
HIGHEST = lax.Precision.HIGHEST
NT = (((1,), (1,)), ((), ()))
NN = (((1,), (0,)), ((), ()))


def split2(x):
    hi = x.astype(jnp.bfloat16)
    lo = (x - hi.astype(jnp.float32)).astype(jnp.bfloat16)
    return hi, lo


def split3(x):
    hi = x.astype(jnp.bfloat16)
    rest = x - hi.astype(jnp.float32)
    mid = rest.astype(jnp.bfloat16)
    lo = (rest - mid.astype(jnp.float32)).astype(jnp.bfloat16)
    return hi, mid, lo


def dot3(a, b, dims):
    ah, al = a
    bh, bl = b
    f = functools.partial(lax.dot_general, dimension_numbers=dims, preferred_element_type=jnp.float32)
    return f(ah, bh) + (f(ah, bl) + f(al, bh))


def cosine(x):
    turns = x * (1.0 / (2.0 * math.pi))
    t = turns - jnp.round(turns)
    u = t * t
    s = SINE[-1]
    for c in SINE[-2::-1]:
        s = s * u + c
    s = s * t
    return 1.0 - 2.0 * (s * s)


def round_up(n, m):
    return -(-n // m) * m


def column_starts(feats, tail):
    starts, at = [], 0
    for j in range(feats // WIDE):
        starts.append(at)
        at += feats - j * WIDE + tail
    return starts, at


def gram_kernel(proj_ref, phase_ref, samples_ref, residual_ref, extra_ref, packed_ref, fh_ref, fl_ref, sh, sl, rh, rl):
    feats = proj_ref.shape[0]
    classes = residual_ref.shape[0]
    tail = rh.shape[0]
    starts, _ = column_starts(feats, tail)
    h, l = split2(samples_ref[...])
    sh[...] = h
    sl[...] = l
    rh[...] = jnp.zeros_like(rh)
    rl[...] = jnp.zeros_like(rl)
    h, l = split2(residual_ref[...])
    rh[0:classes, :] = h
    rl[0:classes, :] = l

    @pl.loop(0, feats // PANEL)
    def _(i):
        rows = pl.ds(pl.multiple_of(i * PANEL, PANEL), PANEL)
        inner = dot3(split2(proj_ref[rows, :]), (sh[...], sl[...]), NN)
        h, l = split2(cosine(inner + phase_ref[rows, :]))
        fh_ref[rows, :] = h
        fl_ref[rows, :] = l

    for j in range(feats // WIDE):
        cols = slice(j * WIDE, (j + 1) * WIDE)

        @pl.loop(j, feats // WIDE)
        def _(i):
            rows = pl.ds(pl.multiple_of(i * WIDE, WIDE), WIDE)
            out = pl.ds(pl.multiple_of(starts[j] + (i - j) * WIDE, 32), WIDE)
            packed_ref[out, :] = dot3((fh_ref[rows, :], fl_ref[rows, :]), (fh_ref[cols, :], fl_ref[cols, :]), NT)

        at = starts[j] + feats - j * WIDE
        right = dot3((rh[...], rl[...]), (fh_ref[cols, :], fl_ref[cols, :]), NT)
        packed_ref[at : at + tail, :] = right
        packed_ref[at : at + classes, :] = right[:classes, :] + extra_ref[:, cols]


def spread_lane(x, lane):
    return jnp.broadcast_to(x[:, lane : lane + 1], x.shape)


def spread_row(x, row):
    return jnp.broadcast_to(x[row : row + 1, :], x.shape)


def inverse_factor(block):
    size = block.shape[0]
    shape = (SUB, size)
    row = lax.broadcasted_iota(jnp.int32, shape, 0)
    lane = lax.broadcasted_iota(jnp.int32, shape, 1)
    tiles = [block[t * SUB : (t + 1) * SUB, :] for t in range(size // SUB)]
    for s in range(size // SUB):
        base = s * SUB
        own = (lane >= base) & (lane < base + SUB)
        columns = [spread_lane(tiles[s], base + c) for c in range(SUB)]
        work = jnp.where(own, jnp.where(lane - base == row, 1.0, 0.0), tiles[s])
        pivots = []
        scale = jnp.zeros(shape, jnp.float32)
        for k in range(SUB):
            pivot_row = spread_row(work, k)
            heads = [spread_row(columns[c], k) for c in range(k, SUB)]
            inv = 1.0 / heads[0]
            scale = jnp.where(row == k, lax.rsqrt(heads[0]), scale)
            if k < SUB - 1:
                m = jnp.where(row > k, columns[k] * inv, 0.0)
                for c in range(k + 1, SUB):
                    columns[c] = columns[c] - m * heads[c - k]
                work = work - m * pivot_row
            pivots.append((inv, pivot_row, heads))
        tiles[s] = work * scale
        for t in range(s + 1, size // SUB):
            columns = [spread_lane(tiles[t], base + c) for c in range(SUB)]
            work = jnp.where(own, 0.0, tiles[t])
            for k, (inv, pivot_row, heads) in enumerate(pivots):
                m = columns[k] * inv
                for c in range(k + 1, SUB):
                    columns[c] = columns[c] - m * heads[c - k]
                work = work - m * pivot_row
            tiles[t] = work
    full = jnp.concatenate(tiles, axis=0)
    keep = lax.broadcasted_iota(jnp.int32, (size, size), 0) >= lax.broadcasted_iota(jnp.int32, (size, size), 1)
    return jnp.where(keep, full, 0.0)


def solve_kernel(total_rows, packed_ref, fh_ref, fl_ref, residual_ref, weights_ref, new_weights_ref, new_residual_ref, aug, linv, left, right, xs):
    feats = fh_ref.shape[0]
    classes = residual_ref.shape[0]
    height = aug.shape[0]
    tail = height - feats
    starts, _ = column_starts(feats, tail)
    panels = feats // PANEL
    diag = lax.broadcasted_iota(jnp.int32, (WIDE, WIDE), 0) == lax.broadcasted_iota(jnp.int32, (WIDE, WIDE), 1)
    for j in range(feats // WIDE):
        c = j * WIDE
        rows = height - c
        aug[c : c + WIDE, c : c + WIDE] = packed_ref[starts[j] : starts[j] + WIDE, :] / total_rows + jnp.where(diag, ridge_weight, 0.0)
        aug[c + WIDE :, c : c + WIDE] = packed_ref[starts[j] + WIDE : starts[j] + rows, :] / total_rows

    @pl.loop(0, panels)
    def _(p):
        at = pl.ds(pl.multiple_of(p * PANEL, PANEL), PANEL)
        inverse = inverse_factor(aug[at, at])
        linv[at, :] = inverse

        for q in range(panels):

            @pl.when(p == q)
            def _():
                c0 = (q + 1) * PANEL
                body = lax.dot_general(
                    aug[c0:, q * PANEL : c0], linv[q * PANEL : c0, :], NT, precision=HIGHEST, preferred_element_type=jnp.float32
                )
                aug[c0:, q * PANEL : c0] = body
                h, m, l = split3(body)
                for i, part in enumerate((h, h, m, h, l, m)):
                    left[c0:, i * PANEL : (i + 1) * PANEL] = part
                n = feats - c0
                if n > 0:
                    for i, part in enumerate((h, m, h, l, h, m)):
                        right[c0:feats, i * PANEL : (i + 1) * PANEL] = part[:n]
                c = c0
                while c < feats:
                    w = PANEL if c % WIDE else WIDE
                    aug[c:, c : c + w] = aug[c:, c : c + w] - lax.dot_general(
                        left[c:, :], right[c : c + w, :], NT, preferred_element_type=jnp.float32
                    )
                    c += w

    for p in reversed(range(panels)):
        c = p * PANEL
        x = lax.dot_general(
            aug[feats:, c : c + PANEL], linv[c : c + PANEL, :], NN, precision=HIGHEST, preferred_element_type=jnp.float32
        )
        xs[:, c : c + PANEL] = x
        if p > 0:
            aug[feats:, 0:c] = aug[feats:, 0:c] - lax.dot_general(
                x, aug[c : c + PANEL, 0:c], NN, precision=HIGHEST, preferred_element_type=jnp.float32
            )

    own = weights_ref.shape[1]
    mine = pl.ds(pl.multiple_of(lax.axis_index("feat") * own, PANEL), own)
    new_weights_ref[...] = weights_ref[...] + xs[0:classes, mine]
    x = split2(xs[...])
    frames = fh_ref.shape[1]

    for c in range(0, frames, WIDE):
        fitted = dot3(x, (fh_ref[:, c : c + WIDE], fl_ref[:, c : c + WIDE]), NN)
        new_residual_ref[:, c : c + WIDE] = residual_ref[:, c : c + WIDE] - fitted[:classes, :]


def per_device(samples, residual, bank, bank_phase, bank_weights, block_index):
    chosen = block_index[0]
    local_projection = lax.dynamic_index_in_dim(bank, chosen, 0, keepdims=False)
    local_phases = lax.dynamic_index_in_dim(bank_phase, chosen, 0, keepdims=True)
    local_weights = lax.dynamic_index_in_dim(bank_weights, chosen, 0, keepdims=False)
    projection = lax.all_gather(local_projection.T, "feat", axis=0, tiled=True)
    phases = lax.all_gather(local_phases, "feat", axis=1, tiled=True).T
    feats, depth = projection.shape
    classes, frames = residual.shape
    total_rows = frames * lax.axis_size("feat") * lax.axis_size("rows")
    own = local_weights.shape[1]
    mine = jnp.where(lax.axis_index("rows") == 0, -ridge_weight * total_rows, 0.0) * local_weights
    extra = lax.dynamic_update_slice(
        jnp.zeros((classes, feats), jnp.float32), mine, (0, lax.axis_index("feat") * own)
    )
    tail = round_up(classes, 32)
    _, packed_rows = column_starts(feats, tail)
    vmem = pl.BlockSpec(memory_space=pltpu.VMEM)
    params = pltpu.CompilerParams(vmem_limit_bytes=50 * 1024 * 1024)
    packed, fh, fl = pl.pallas_call(
        gram_kernel,
        out_shape=(
            jax.ShapeDtypeStruct((packed_rows, WIDE), jnp.float32),
            jax.ShapeDtypeStruct((feats, frames), jnp.bfloat16),
            jax.ShapeDtypeStruct((feats, frames), jnp.bfloat16),
        ),
        in_specs=[vmem] * 5,
        out_specs=(vmem,) * 3,
        scratch_shapes=[
            pltpu.VMEM((depth, frames), jnp.bfloat16),
            pltpu.VMEM((depth, frames), jnp.bfloat16),
            pltpu.VMEM((tail, frames), jnp.bfloat16),
            pltpu.VMEM((tail, frames), jnp.bfloat16),
        ],
        compiler_params=params,
        name="features_gram",
    )(projection, phases, samples, residual, extra)
    packed = lax.psum(packed, ("feat", "rows"))
    new_weights, new_residual = pl.pallas_call(
        functools.partial(solve_kernel, total_rows),
        out_shape=(
            jax.ShapeDtypeStruct(local_weights.shape, jnp.float32),
            jax.ShapeDtypeStruct(residual.shape, jnp.float32),
        ),
        in_specs=[vmem] * 5,
        out_specs=(vmem,) * 2,
        scratch_shapes=[
            pltpu.VMEM((feats + tail, feats), jnp.float32),
            pltpu.VMEM((feats, PANEL), jnp.float32),
            pltpu.VMEM((feats + tail, 6 * PANEL), jnp.bfloat16),
            pltpu.VMEM((feats, 6 * PANEL), jnp.bfloat16),
            pltpu.VMEM((tail, feats), jnp.float32),
        ],
        compiler_params=params,
        name="solve_fit",
    )(packed, fh, fl, residual, local_weights)
    return (new_weights, new_residual)


def solution(mesh):
    in_specs = (
        P(None, ("feat", "rows")),
        P(None, ("feat", "rows")),
        P(None, None, "feat"),
        P(None, "feat"),
        P(None, None, "feat"),
        P(),
    )
    out_specs = (P(None, "feat"), P(None, ("feat", "rows")))
    return jax.shard_map(
        per_device, mesh=mesh, in_specs=in_specs, out_specs=out_specs, check_vma=False
    )
```

```python
import functools
import math

import jax
import jax.numpy as jnp
from jax import lax
from jax.experimental import pallas as pl
from jax.experimental.pallas import tpu as pltpu
from jax.sharding import PartitionSpec as P

ridge_weight = 0.05
WIDE = 256
PANEL = 128
SUB = 8
SINE = (3.141592640144165, -5.167710084047848, 2.550077528428822, -0.598291299770303, 0.07765766117753167)
HIGHEST = lax.Precision.HIGHEST
NT = (((1,), (1,)), ((), ()))
NN = (((1,), (0,)), ((), ()))


def split2(x):
    hi = x.astype(jnp.bfloat16)
    lo = (x - hi.astype(jnp.float32)).astype(jnp.bfloat16)
    return hi, lo


def split3(x):
    hi = x.astype(jnp.bfloat16)
    rest = x - hi.astype(jnp.float32)
    mid = rest.astype(jnp.bfloat16)
    lo = (rest - mid.astype(jnp.float32)).astype(jnp.bfloat16)
    return hi, mid, lo


def dot3(a, b, dims):
    ah, al = a
    bh, bl = b
    f = functools.partial(lax.dot_general, dimension_numbers=dims, preferred_element_type=jnp.float32)
    return f(ah, bh) + (f(ah, bl) + f(al, bh))


def cosine(x):
    turns = x * (1.0 / (2.0 * math.pi))
    t = turns - jnp.round(turns)
    u = t * t
    s = SINE[-1]
    for c in SINE[-2::-1]:
        s = s * u + c
    s = s * t
    return 1.0 - 2.0 * (s * s)


def round_up(n, m):
    return -(-n // m) * m


def panel_starts(feats, tail):
    starts, at = [], 0
    for p in range(feats // PANEL):
        starts.append(at)
        at += feats - p * PANEL + tail
    return starts, at


def gram_kernel(proj_ref, phase_ref, samples_ref, residual_ref, extra_ref, packed_ref, fh_ref, fl_ref, sh, sl, rh, rl):
    feats = proj_ref.shape[0]
    classes = residual_ref.shape[0]
    tail = rh.shape[0]
    starts, used = panel_starts(feats, tail)
    packed_ref[used:, :] = jnp.zeros_like(packed_ref[used:, :])
    h, l = split2(samples_ref[...])
    sh[...] = h
    sl[...] = l
    rh[...] = jnp.zeros_like(rh)
    rl[...] = jnp.zeros_like(rl)
    h, l = split2(residual_ref[...])
    rh[0:classes, :] = h
    rl[0:classes, :] = l

    @pl.loop(0, feats // PANEL)
    def _(i):
        rows = pl.ds(pl.multiple_of(i * PANEL, PANEL), PANEL)
        inner = dot3(split2(proj_ref[rows, :]), (sh[...], sl[...]), NN)
        h, l = split2(cosine(inner + phase_ref[rows, :]))
        fh_ref[rows, :] = h
        fl_ref[rows, :] = l

    for j in range(feats // WIDE):
        cols = slice(j * WIDE, (j + 1) * WIDE)
        even, odd = starts[2 * j], starts[2 * j + 1]
        other = (fh_ref[cols, :], fl_ref[cols, :])
        block = dot3(other, other, NT)
        packed_ref[even : even + WIDE, :] = block[:, :PANEL]
        packed_ref[odd : odd + PANEL, :] = block[PANEL:, PANEL:]

        @pl.loop(j + 1, feats // WIDE)
        def _(i):
            rows = pl.ds(pl.multiple_of(i * WIDE, WIDE), WIDE)
            below = (i - j) * WIDE
            block = dot3((fh_ref[rows, :], fl_ref[rows, :]), (fh_ref[cols, :], fl_ref[cols, :]), NT)
            packed_ref[pl.ds(pl.multiple_of(even + below, 32), WIDE), :] = block[:, :PANEL]
            packed_ref[pl.ds(pl.multiple_of(odd + below - PANEL, 32), WIDE), :] = block[:, PANEL:]

        right = dot3((rh[...], rl[...]), (fh_ref[cols, :], fl_ref[cols, :]), NT)
        for half, start in enumerate((even, odd)):
            c = j * WIDE + half * PANEL
            at = start + feats - c
            part = right[:, half * PANEL : (half + 1) * PANEL]
            packed_ref[at : at + tail, :] = part
            packed_ref[at : at + classes, :] = part[:classes, :] + extra_ref[:, c : c + PANEL]


def sum_stages(n_feat, n_rows, inner):
    return {
        "core": ("feat", 2, 1),
        "x": ("feat", n_feat // 2, 2),
        "near": ("rows", inner, 1),
        "far": ("rows", n_rows // inner, inner),
    }


PIECES = 4
ORDERS = (("core", "x", "near", "far"), ("core", "near", "x", "far"))


def slot_rows(rows, stages):
    sizes = []
    for order in ORDERS:
        n, line = rows, []
        for name in order:
            n //= stages[name][1]
            line.append(n)
        sizes.append(line)
    return sizes


def sum_kernel(stages, in_ref, out_ref, acc, *scratch):
    depth = len(ORDERS[0])
    slots, recv_sems, send_sems = scratch[: 2 * depth], scratch[2 * depth : 4 * depth], scratch[4 * depth :]
    piece_rows = in_ref.shape[0] // PIECES
    index = {"feat": lax.axis_index("feat"), "rows": lax.axis_index("rows")}
    place, peers = {}, {}
    for name, (axis, size, stride) in stages.items():
        here = lax.rem(lax.div(index[axis], stride), size)
        place[name] = here
        peers[name] = []
        for d in range(1, size):
            there = lax.rem(here + d, size)
            target = index[axis] + (there - here) * stride
            ids = (target, index["rows"]) if axis == "feat" else (index["feat"], target)
            peers[name].append((there, ids))

    barrier = pltpu.get_barrier_semaphore()
    count = 0
    for name in stages:
        for _, ids in peers[name]:
            pl.semaphore_signal(barrier, inc=1, device_id=ids, device_id_type=pl.DeviceIdType.MESH)
            count += 1
    pl.semaphore_wait(barrier, count)

    sends = []
    sizes = slot_rows(piece_rows, stages)
    bases = []
    for piece in range(PIECES):
        base, line = piece * piece_rows, [piece * piece_rows]
        for level, name in enumerate(ORDERS[piece % 2]):
            base = base + place[name] * sizes[piece % 2][level]
            line.append(base)
        bases.append(line)

    def rows_at(start, n):
        return pl.ds(pl.multiple_of(start, 8), n)

    def start_reduce(piece, level):
        kind = piece % 2
        name, n = ORDERS[kind][level], sizes[kind][level]
        source = in_ref if level == 0 else acc
        copies = []
        for d, (there, ids) in enumerate(peers[name]):
            which = 2 * level + kind
            copy = pltpu.make_async_remote_copy(
                src_ref=source.at[rows_at(bases[piece][level] + there * n, n)],
                dst_ref=slots[which].at[piece // 2, d],
                send_sem=send_sems[which].at[0, piece // 2, d],
                recv_sem=recv_sems[which].at[0, piece // 2, d],
                device_id=ids,
                device_id_type=pl.DeviceIdType.MESH,
            )
            copy.start()
            copies.append(copy)
            sends.append(copy)
        return copies

    def end_reduce(piece, level, copies):
        kind = piece % 2
        n = sizes[kind][level]
        source = in_ref if level == 0 else acc
        target = out_ref if level == depth - 1 else acc
        mine = rows_at(bases[piece][level + 1], n)
        total = source[mine, :]
        for d, copy in enumerate(copies):
            copy.wait_recv()
            total = total + slots[2 * level + kind][piece // 2, d]
        target[mine, :] = total

    def start_gather(piece, level):
        kind = piece % 2
        name, n = ORDERS[kind][level], sizes[kind][level]
        mine = rows_at(bases[piece][level + 1], n)
        copies = []
        for d, (_, ids) in enumerate(peers[name]):
            which = 2 * level + kind
            copy = pltpu.make_async_remote_copy(
                src_ref=out_ref.at[mine],
                dst_ref=out_ref.at[mine],
                send_sem=send_sems[which].at[1, piece // 2, d],
                recv_sem=recv_sems[which].at[1, piece // 2, d],
                device_id=ids,
                device_id_type=pl.DeviceIdType.MESH,
            )
            copy.start()
            copies.append(copy)
            sends.append(copy)
        return copies

    flying = [start_reduce(piece, 0) for piece in range(PIECES)]
    for level in range(depth):
        for piece in range(PIECES):
            end_reduce(piece, level, flying[piece])
            if level + 1 < depth:
                flying[piece] = start_reduce(piece, level + 1)
            else:
                flying[piece] = start_gather(piece, level)
    for level in reversed(range(depth)):
        for piece in range(PIECES):
            for copy in flying[piece]:
                copy.wait_recv()
            if level > 0:
                flying[piece] = start_gather(piece, level - 1)
    for copy in sends:
        copy.wait_send()


def sum_everywhere(packed, stages):
    rows, width = packed.shape
    depth = len(ORDERS[0])
    sizes = slot_rows(rows // PIECES, stages)
    slots, sems = [], []
    for level in range(depth):
        for kind in range(2):
            others = max(stages[ORDERS[kind][level]][1] - 1, 1)
            slots.append(pltpu.VMEM((PIECES // 2, others, sizes[kind][level], width), jnp.float32))
            sems.append(pltpu.SemaphoreType.DMA((2, PIECES // 2, others)))
    vmem = pl.BlockSpec(memory_space=pltpu.VMEM)
    return pl.pallas_call(
        functools.partial(sum_kernel, stages),
        out_shape=jax.ShapeDtypeStruct(packed.shape, packed.dtype),
        in_specs=[vmem],
        out_specs=vmem,
        scratch_shapes=[pltpu.VMEM(packed.shape, packed.dtype)] + slots + sems + sems,
        compiler_params=pltpu.CompilerParams(
            vmem_limit_bytes=50 * 1024 * 1024, collective_id=0, has_side_effects=True
        ),
        name="sum_everywhere",
    )(packed)


def spread_lane(x, lane):
    return jnp.broadcast_to(x[:, lane : lane + 1], x.shape)


def spread_row(x, row):
    return jnp.broadcast_to(x[row : row + 1, :], x.shape)


def inverse_factor(block):
    size = block.shape[0]
    shape = (SUB, size)
    row = lax.broadcasted_iota(jnp.int32, shape, 0)
    lane = lax.broadcasted_iota(jnp.int32, shape, 1)
    tiles = [block[t * SUB : (t + 1) * SUB, :] for t in range(size // SUB)]
    for s in range(size // SUB):
        base = s * SUB
        own = (lane >= base) & (lane < base + SUB)
        columns = [spread_lane(tiles[s], base + c) for c in range(SUB)]
        work = jnp.where(own, jnp.where(lane - base == row, 1.0, 0.0), tiles[s])
        pivots = []
        scale = jnp.zeros(shape, jnp.float32)
        for k in range(SUB):
            pivot_row = spread_row(work, k)
            heads = [spread_row(columns[c], k) for c in range(k, SUB)]
            inv = 1.0 / heads[0]
            scale = jnp.where(row == k, lax.rsqrt(heads[0]), scale)
            if k < SUB - 1:
                m = jnp.where(row > k, columns[k] * inv, 0.0)
                for c in range(k + 1, SUB):
                    columns[c] = columns[c] - m * heads[c - k]
                work = work - m * pivot_row
            pivots.append((inv, pivot_row, heads))
        tiles[s] = work * scale
        for t in range(s + 1, size // SUB):
            columns = [spread_lane(tiles[t], base + c) for c in range(SUB)]
            work = jnp.where(own, 0.0, tiles[t])
            for k, (inv, pivot_row, heads) in enumerate(pivots):
                m = columns[k] * inv
                for c in range(k + 1, SUB):
                    columns[c] = columns[c] - m * heads[c - k]
                work = work - m * pivot_row
            tiles[t] = work
    full = jnp.concatenate(tiles, axis=0)
    keep = lax.broadcasted_iota(jnp.int32, (size, size), 0) >= lax.broadcasted_iota(jnp.int32, (size, size), 1)
    return jnp.where(keep, full, 0.0)


def solve_kernel(total_rows, packed_ref, fh_ref, fl_ref, residual_ref, weights_ref, new_weights_ref, new_residual_ref, aug, linv, left, right, xs):
    feats = fh_ref.shape[0]
    classes = residual_ref.shape[0]
    height = aug.shape[0]
    tail = height - feats
    starts, _ = panel_starts(feats, tail)
    panels = feats // PANEL
    diag = lax.broadcasted_iota(jnp.int32, (PANEL, PANEL), 0) == lax.broadcasted_iota(jnp.int32, (PANEL, PANEL), 1)
    for p in range(panels):
        c = p * PANEL
        at = starts[p]
        aug[c : c + PANEL, c : c + PANEL] = packed_ref[at : at + PANEL, :] / total_rows + jnp.where(diag, ridge_weight, 0.0)
        aug[c + PANEL :, c : c + PANEL] = packed_ref[at + PANEL : at + height - c, :] / total_rows

    @pl.loop(0, panels)
    def _(p):
        at = pl.ds(pl.multiple_of(p * PANEL, PANEL), PANEL)
        inverse = inverse_factor(aug[at, at])
        linv[at, :] = inverse

        for q in range(panels):

            @pl.when(p == q)
            def _():
                c0 = (q + 1) * PANEL
                body = lax.dot_general(
                    aug[c0:, q * PANEL : c0], linv[q * PANEL : c0, :], NT, precision=HIGHEST, preferred_element_type=jnp.float32
                )
                aug[c0:, q * PANEL : c0] = body
                h, m, l = split3(body)
                for i, part in enumerate((h, h, m, h, l, m)):
                    left[c0:, i * PANEL : (i + 1) * PANEL] = part
                n = feats - c0
                if n > 0:
                    for i, part in enumerate((h, m, h, l, h, m)):
                        right[c0:feats, i * PANEL : (i + 1) * PANEL] = part[:n]
                c = c0
                while c < feats:
                    w = PANEL if c % WIDE else WIDE
                    aug[c:, c : c + w] = aug[c:, c : c + w] - lax.dot_general(
                        left[c:, :], right[c : c + w, :], NT, preferred_element_type=jnp.float32
                    )
                    c += w

    for p in reversed(range(panels)):
        c = p * PANEL
        x = lax.dot_general(
            aug[feats:, c : c + PANEL], linv[c : c + PANEL, :], NN, precision=HIGHEST, preferred_element_type=jnp.float32
        )
        xs[:, c : c + PANEL] = x
        if p > 0:
            aug[feats:, 0:c] = aug[feats:, 0:c] - lax.dot_general(
                x, aug[c : c + PANEL, 0:c], NN, precision=HIGHEST, preferred_element_type=jnp.float32
            )

    own = weights_ref.shape[1]
    mine = pl.ds(pl.multiple_of(lax.axis_index("feat") * own, PANEL), own)
    new_weights_ref[...] = weights_ref[...] + xs[0:classes, mine]
    x = split2(xs[...])
    frames = fh_ref.shape[1]

    for c in range(0, frames, WIDE):
        fitted = dot3(x, (fh_ref[:, c : c + WIDE], fl_ref[:, c : c + WIDE]), NN)
        new_residual_ref[:, c : c + WIDE] = residual_ref[:, c : c + WIDE] - fitted[:classes, :]


def per_device(inner, samples, residual, bank, bank_phase, bank_weights, block_index):
    chosen = block_index[0]
    local_projection = lax.dynamic_index_in_dim(bank, chosen, 0, keepdims=False)
    local_phases = lax.dynamic_index_in_dim(bank_phase, chosen, 0, keepdims=True)
    local_weights = lax.dynamic_index_in_dim(bank_weights, chosen, 0, keepdims=False)
    projection = lax.all_gather(local_projection.T, "feat", axis=0, tiled=True)
    phases = lax.all_gather(local_phases, "feat", axis=1, tiled=True).T
    feats, depth = projection.shape
    classes, frames = residual.shape
    total_rows = frames * lax.axis_size("feat") * lax.axis_size("rows")
    own = local_weights.shape[1]
    mine = jnp.where(lax.axis_index("rows") == 0, -ridge_weight * total_rows, 0.0) * local_weights
    extra = lax.dynamic_update_slice(
        jnp.zeros((classes, feats), jnp.float32), mine, (0, lax.axis_index("feat") * own)
    )
    tail = round_up(classes, 32)
    n_feat, n_rows = lax.axis_size("feat"), lax.axis_size("rows")
    packed_rows = round_up(panel_starts(feats, tail)[1], PIECES * n_feat * n_rows * 8)
    vmem = pl.BlockSpec(memory_space=pltpu.VMEM)
    params = pltpu.CompilerParams(vmem_limit_bytes=50 * 1024 * 1024)
    packed, fh, fl = pl.pallas_call(
        gram_kernel,
        out_shape=(
            jax.ShapeDtypeStruct((packed_rows, PANEL), jnp.float32),
            jax.ShapeDtypeStruct((feats, frames), jnp.bfloat16),
            jax.ShapeDtypeStruct((feats, frames), jnp.bfloat16),
        ),
        in_specs=[vmem] * 5,
        out_specs=(vmem,) * 3,
        scratch_shapes=[
            pltpu.VMEM((depth, frames), jnp.bfloat16),
            pltpu.VMEM((depth, frames), jnp.bfloat16),
            pltpu.VMEM((tail, frames), jnp.bfloat16),
            pltpu.VMEM((tail, frames), jnp.bfloat16),
        ],
        compiler_params=params,
        name="features_gram",
    )(projection, phases, samples, residual, extra)
    packed = sum_everywhere(packed, sum_stages(n_feat, n_rows, inner))
    new_weights, new_residual = pl.pallas_call(
        functools.partial(solve_kernel, total_rows),
        out_shape=(
            jax.ShapeDtypeStruct(local_weights.shape, jnp.float32),
            jax.ShapeDtypeStruct(residual.shape, jnp.float32),
        ),
        in_specs=[vmem] * 5,
        out_specs=(vmem,) * 2,
        scratch_shapes=[
            pltpu.VMEM((feats + tail, feats), jnp.float32),
            pltpu.VMEM((feats, PANEL), jnp.float32),
            pltpu.VMEM((feats + tail, 6 * PANEL), jnp.bfloat16),
            pltpu.VMEM((feats, 6 * PANEL), jnp.bfloat16),
            pltpu.VMEM((tail, feats), jnp.float32),
        ],
        compiler_params=params,
        name="solve_fit",
    )(packed, fh, fl, residual, local_weights)
    return (new_weights, new_residual)


def near_size(devices):
    line = [getattr(d, "coords", None) for d in devices[0]]
    if any(c is None for c in line):
        return 2
    moved = [tuple(a != b for a, b in zip(c, line[0])) for c in line]
    for r in range(2, len(line)):
        if moved[r] != moved[1]:
            return r
    return len(line)


def solution(mesh):
    in_specs = (
        P(None, ("feat", "rows")),
        P(None, ("feat", "rows")),
        P(None, None, "feat"),
        P(None, "feat"),
        P(None, None, "feat"),
        P(),
    )
    out_specs = (P(None, "feat"), P(None, ("feat", "rows")))
    return jax.shard_map(
        functools.partial(per_device, near_size(mesh.devices)), mesh=mesh, in_specs=in_specs, out_specs=out_specs, check_vma=False
    )
```

```python
import functools
import math

import jax
import jax.numpy as jnp
from jax import lax
from jax.experimental import pallas as pl
from jax.experimental.pallas import tpu as pltpu
from jax.sharding import PartitionSpec as P

ridge_weight = 0.05
WIDE = 256
PANEL = 128
SUB = 8
SINE = (3.141592640144165, -5.167710084047848, 2.550077528428822, -0.598291299770303, 0.07765766117753167)
HIGHEST = lax.Precision.HIGHEST
NT = (((1,), (1,)), ((), ()))
NN = (((1,), (0,)), ((), ()))


def split2(x):
    hi = x.astype(jnp.bfloat16)
    lo = (x - hi.astype(jnp.float32)).astype(jnp.bfloat16)
    return hi, lo


def split3(x):
    hi = x.astype(jnp.bfloat16)
    rest = x - hi.astype(jnp.float32)
    mid = rest.astype(jnp.bfloat16)
    lo = (rest - mid.astype(jnp.float32)).astype(jnp.bfloat16)
    return hi, mid, lo


def dot3(a, b, dims):
    ah, al = a
    bh, bl = b
    f = functools.partial(lax.dot_general, dimension_numbers=dims, preferred_element_type=jnp.float32)
    return f(ah, bh) + (f(ah, bl) + f(al, bh))


def cosine(x):
    turns = x * (1.0 / (2.0 * math.pi))
    t = turns - jnp.round(turns)
    u = t * t
    s = SINE[-1]
    for c in SINE[-2::-1]:
        s = s * u + c
    s = s * t
    return 1.0 - 2.0 * (s * s)


def round_up(n, m):
    return -(-n // m) * m


def panel_starts(feats, tail):
    starts, at = [], 0
    for p in range(feats // PANEL):
        starts.append(at)
        at += feats - p * PANEL + tail
    return starts, at


def gram_kernel(
    depth, own_ref, samples_ref, residual_ref, extra_ref, packed_ref, fh_ref, fl_ref, bank, sh, sl, rh, rl, *sems
):
    core_send, core_recv, x_send, x_recv, pass_send, pass_recv = sems
    feats = fh_ref.shape[0]
    classes = residual_ref.shape[0]
    tail = rh.shape[0]
    n_feat, halves = bank.shape[:2]
    n_x = n_feat // 2
    me, line = lax.axis_index("feat"), lax.axis_index("rows")
    core, x = lax.rem(me, 2), lax.div(me, 2)
    sibling = me + 1 - 2 * core
    after = [lax.rem(x + d, n_x) * 2 + core for d in range(1, n_x)]
    before = [lax.rem(x + n_x - d, n_x) * 2 + core for d in range(1, n_x)]

    barrier = pltpu.get_barrier_semaphore()
    for other in [sibling] + after:
        pl.semaphore_signal(barrier, inc=1, device_id=(other, line), device_id_type=pl.DeviceIdType.MESH)
    pl.semaphore_wait(barrier, n_x)

    def send(source, slot, half, send_sem, recv_sem, other):
        copy = pltpu.make_async_remote_copy(
            src_ref=source,
            dst_ref=bank.at[slot, half],
            send_sem=send_sem,
            recv_sem=recv_sem,
            device_id=(other, line),
            device_id_type=pl.DeviceIdType.MESH,
        )
        copy.start()
        return copy

    def own_half(half):
        return own_ref.at[:, half * PANEL : (half + 1) * PANEL]

    across, beside, passed = {}, {}, {}
    for half in range(halves):
        for d, other in enumerate(after):
            across[d, half] = send(own_half(half), me, half, x_send.at[d, half], x_recv.at[d, half], other)
    for half in range(halves):
        beside[half] = send(own_half(half), me, half, core_send.at[half], core_recv.at[half], sibling)

    starts, used = panel_starts(feats, tail)
    packed_ref[used:, :] = jnp.zeros_like(packed_ref[used:, :])
    h, l = split2(samples_ref[...])
    sh[...] = h
    sl[...] = l
    rh[...] = jnp.zeros_like(rh)
    rl[...] = jnp.zeros_like(rl)
    h, l = split2(residual_ref[...])
    rh[0:classes, :] = h
    rl[0:classes, :] = l

    def make_features(part, shard, half):
        turned = part.T
        inner = dot3(split2(turned[:, :depth]), (sh[...], sl[...]), NN)
        h, l = split2(cosine(inner + turned[:, depth : depth + 1]))
        rows = pl.ds(pl.multiple_of((shard * halves + half) * PANEL, PANEL), PANEL)
        fh_ref[rows, :] = h
        fl_ref[rows, :] = l

    for half in range(halves):
        make_features(own_ref[:, half * PANEL : (half + 1) * PANEL], me, half)
    for half in range(halves):
        beside[half].wait_recv()
        make_features(bank[sibling, half], sibling, half)
    for half in range(halves):
        for d, shard in enumerate(before):
            across[d, half].wait_recv()
            passed[d, half] = send(
                bank.at[shard, half], shard, half, pass_send.at[d, half], pass_recv.at[d, half], sibling
            )
            make_features(bank[shard, half], shard, half)
            passed[d, half].wait_recv()
            far = shard + 1 - 2 * core
            make_features(bank[far, half], far, half)
    for copies in (across, beside, passed):
        for copy in copies.values():
            copy.wait_send()

    for j in range(feats // WIDE):
        cols = slice(j * WIDE, (j + 1) * WIDE)
        even, odd = starts[2 * j], starts[2 * j + 1]
        other = (fh_ref[cols, :], fl_ref[cols, :])
        block = dot3(other, other, NT)
        packed_ref[even : even + WIDE, :] = block[:, :PANEL]
        packed_ref[odd : odd + PANEL, :] = block[PANEL:, PANEL:]

        @pl.loop(j + 1, feats // WIDE)
        def _(i):
            rows = pl.ds(pl.multiple_of(i * WIDE, WIDE), WIDE)
            below = (i - j) * WIDE
            block = dot3((fh_ref[rows, :], fl_ref[rows, :]), (fh_ref[cols, :], fl_ref[cols, :]), NT)
            packed_ref[pl.ds(pl.multiple_of(even + below, 32), WIDE), :] = block[:, :PANEL]
            packed_ref[pl.ds(pl.multiple_of(odd + below - PANEL, 32), WIDE), :] = block[:, PANEL:]

        right = dot3((rh[...], rl[...]), (fh_ref[cols, :], fl_ref[cols, :]), NT)
        for half, start in enumerate((even, odd)):
            c = j * WIDE + half * PANEL
            at = start + feats - c
            part = right[:, half * PANEL : (half + 1) * PANEL]
            packed_ref[at : at + tail, :] = part
            packed_ref[at : at + classes, :] = part[:classes, :] + extra_ref[:, c : c + PANEL]


def sum_stages(n_feat, n_rows, inner):
    return {
        "core": ("feat", 2, 1),
        "x": ("feat", n_feat // 2, 2),
        "near": ("rows", inner, 1),
        "far": ("rows", n_rows // inner, inner),
    }


PIECES = 4
ORDERS = (("core", "x", "near", "far"), ("core", "near", "x", "far"))


def slot_rows(rows, stages):
    sizes = []
    for order in ORDERS:
        n, line = rows, []
        for name in order:
            n //= stages[name][1]
            line.append(n)
        sizes.append(line)
    return sizes


def sum_kernel(stages, in_ref, out_ref, acc, *scratch):
    depth = len(ORDERS[0])
    slots, recv_sems, send_sems = scratch[: 2 * depth], scratch[2 * depth : 4 * depth], scratch[4 * depth :]
    piece_rows = in_ref.shape[0] // PIECES
    index = {"feat": lax.axis_index("feat"), "rows": lax.axis_index("rows")}
    place, peers = {}, {}
    for name, (axis, size, stride) in stages.items():
        here = lax.rem(lax.div(index[axis], stride), size)
        place[name] = here
        peers[name] = []
        for d in range(1, size):
            there = lax.rem(here + d, size)
            target = index[axis] + (there - here) * stride
            ids = (target, index["rows"]) if axis == "feat" else (index["feat"], target)
            peers[name].append((there, ids))

    barrier = pltpu.get_barrier_semaphore()
    count = 0
    for name in stages:
        for _, ids in peers[name]:
            pl.semaphore_signal(barrier, inc=1, device_id=ids, device_id_type=pl.DeviceIdType.MESH)
            count += 1
    pl.semaphore_wait(barrier, count)

    sends = []
    sizes = slot_rows(piece_rows, stages)
    bases = []
    for piece in range(PIECES):
        base, line = piece * piece_rows, [piece * piece_rows]
        for level, name in enumerate(ORDERS[piece % 2]):
            base = base + place[name] * sizes[piece % 2][level]
            line.append(base)
        bases.append(line)

    def rows_at(start, n):
        return pl.ds(pl.multiple_of(start, 8), n)

    def start_reduce(piece, level):
        kind = piece % 2
        name, n = ORDERS[kind][level], sizes[kind][level]
        source = in_ref if level == 0 else acc
        copies = []
        for d, (there, ids) in enumerate(peers[name]):
            which = 2 * level + kind
            copy = pltpu.make_async_remote_copy(
                src_ref=source.at[rows_at(bases[piece][level] + there * n, n)],
                dst_ref=slots[which].at[piece // 2, d],
                send_sem=send_sems[which].at[0, piece // 2, d],
                recv_sem=recv_sems[which].at[0, piece // 2, d],
                device_id=ids,
                device_id_type=pl.DeviceIdType.MESH,
            )
            copy.start()
            copies.append(copy)
            sends.append(copy)
        return copies

    def end_reduce(piece, level, copies):
        kind = piece % 2
        n = sizes[kind][level]
        source = in_ref if level == 0 else acc
        target = out_ref if level == depth - 1 else acc
        mine = rows_at(bases[piece][level + 1], n)
        total = source[mine, :]
        for d, copy in enumerate(copies):
            copy.wait_recv()
            total = total + slots[2 * level + kind][piece // 2, d]
        target[mine, :] = total

    def start_gather(piece, level):
        kind = piece % 2
        name, n = ORDERS[kind][level], sizes[kind][level]
        mine = rows_at(bases[piece][level + 1], n)
        copies = []
        for d, (_, ids) in enumerate(peers[name]):
            which = 2 * level + kind
            copy = pltpu.make_async_remote_copy(
                src_ref=out_ref.at[mine],
                dst_ref=out_ref.at[mine],
                send_sem=send_sems[which].at[1, piece // 2, d],
                recv_sem=recv_sems[which].at[1, piece // 2, d],
                device_id=ids,
                device_id_type=pl.DeviceIdType.MESH,
            )
            copy.start()
            copies.append(copy)
            sends.append(copy)
        return copies

    flying = [start_reduce(piece, 0) for piece in range(PIECES)]
    for level in range(depth):
        for piece in range(PIECES):
            end_reduce(piece, level, flying[piece])
            if level + 1 < depth:
                flying[piece] = start_reduce(piece, level + 1)
            else:
                flying[piece] = start_gather(piece, level)
    for level in reversed(range(depth)):
        for piece in range(PIECES):
            for copy in flying[piece]:
                copy.wait_recv()
            if level > 0:
                flying[piece] = start_gather(piece, level - 1)
    for copy in sends:
        copy.wait_send()


def sum_everywhere(packed, stages):
    rows, width = packed.shape
    depth = len(ORDERS[0])
    sizes = slot_rows(rows // PIECES, stages)
    slots, sems = [], []
    for level in range(depth):
        for kind in range(2):
            others = max(stages[ORDERS[kind][level]][1] - 1, 1)
            slots.append(pltpu.VMEM((PIECES // 2, others, sizes[kind][level], width), jnp.float32))
            sems.append(pltpu.SemaphoreType.DMA((2, PIECES // 2, others)))
    vmem = pl.BlockSpec(memory_space=pltpu.VMEM)
    return pl.pallas_call(
        functools.partial(sum_kernel, stages),
        out_shape=jax.ShapeDtypeStruct(packed.shape, packed.dtype),
        in_specs=[vmem],
        out_specs=vmem,
        scratch_shapes=[pltpu.VMEM(packed.shape, packed.dtype)] + slots + sems + sems,
        compiler_params=pltpu.CompilerParams(
            vmem_limit_bytes=50 * 1024 * 1024, collective_id=0, has_side_effects=True
        ),
        name="sum_everywhere",
    )(packed)


def spread_lane(x, lane):
    return jnp.broadcast_to(x[:, lane : lane + 1], x.shape)


def spread_row(x, row):
    return jnp.broadcast_to(x[row : row + 1, :], x.shape)


def inverse_factor(block):
    size = block.shape[0]
    shape = (SUB, size)
    row = lax.broadcasted_iota(jnp.int32, shape, 0)
    lane = lax.broadcasted_iota(jnp.int32, shape, 1)
    tiles = [block[t * SUB : (t + 1) * SUB, :] for t in range(size // SUB)]
    for s in range(size // SUB):
        base = s * SUB
        own = (lane >= base) & (lane < base + SUB)
        columns = [spread_lane(tiles[s], base + c) for c in range(SUB)]
        work = jnp.where(own, jnp.where(lane - base == row, 1.0, 0.0), tiles[s])
        pivots = []
        scale = jnp.zeros(shape, jnp.float32)
        for k in range(SUB):
            pivot_row = spread_row(work, k)
            heads = [spread_row(columns[c], k) for c in range(k, SUB)]
            inv = 1.0 / heads[0]
            scale = jnp.where(row == k, lax.rsqrt(heads[0]), scale)
            if k < SUB - 1:
                m = jnp.where(row > k, columns[k] * inv, 0.0)
                for c in range(k + 1, SUB):
                    columns[c] = columns[c] - m * heads[c - k]
                work = work - m * pivot_row
            pivots.append((inv, pivot_row, heads))
        tiles[s] = work * scale
        for t in range(s + 1, size // SUB):
            columns = [spread_lane(tiles[t], base + c) for c in range(SUB)]
            work = jnp.where(own, 0.0, tiles[t])
            for k, (inv, pivot_row, heads) in enumerate(pivots):
                m = columns[k] * inv
                for c in range(k + 1, SUB):
                    columns[c] = columns[c] - m * heads[c - k]
                work = work - m * pivot_row
            tiles[t] = work
    full = jnp.concatenate(tiles, axis=0)
    keep = lax.broadcasted_iota(jnp.int32, (size, size), 0) >= lax.broadcasted_iota(jnp.int32, (size, size), 1)
    return jnp.where(keep, full, 0.0)


def solve_kernel(total_rows, packed_ref, fh_ref, fl_ref, residual_ref, weights_ref, new_weights_ref, new_residual_ref, aug, linv, left, right, xs):
    feats = fh_ref.shape[0]
    classes = residual_ref.shape[0]
    height = aug.shape[0]
    tail = height - feats
    starts, _ = panel_starts(feats, tail)
    panels = feats // PANEL
    diag = lax.broadcasted_iota(jnp.int32, (PANEL, PANEL), 0) == lax.broadcasted_iota(jnp.int32, (PANEL, PANEL), 1)
    for p in range(panels):
        c = p * PANEL
        at = starts[p]
        aug[c : c + PANEL, c : c + PANEL] = packed_ref[at : at + PANEL, :] / total_rows + jnp.where(diag, ridge_weight, 0.0)
        aug[c + PANEL :, c : c + PANEL] = packed_ref[at + PANEL : at + height - c, :] / total_rows

    @pl.loop(0, panels)
    def _(p):
        at = pl.ds(pl.multiple_of(p * PANEL, PANEL), PANEL)
        inverse = inverse_factor(aug[at, at])
        linv[at, :] = inverse

        for q in range(panels):

            @pl.when(p == q)
            def _():
                c0 = (q + 1) * PANEL
                body = lax.dot_general(
                    aug[c0:, q * PANEL : c0], linv[q * PANEL : c0, :], NT, precision=HIGHEST, preferred_element_type=jnp.float32
                )
                aug[c0:, q * PANEL : c0] = body
                h, m, l = split3(body)
                for i, part in enumerate((h, h, m, h, l, m)):
                    left[c0:, i * PANEL : (i + 1) * PANEL] = part
                n = feats - c0
                if n > 0:
                    for i, part in enumerate((h, m, h, l, h, m)):
                        right[c0:feats, i * PANEL : (i + 1) * PANEL] = part[:n]
                c = c0
                while c < feats:
                    w = PANEL if c % WIDE else WIDE
                    aug[c:, c : c + w] = aug[c:, c : c + w] - lax.dot_general(
                        left[c:, :], right[c : c + w, :], NT, preferred_element_type=jnp.float32
                    )
                    c += w

    for p in reversed(range(panels)):
        c = p * PANEL
        x = lax.dot_general(
            aug[feats:, c : c + PANEL], linv[c : c + PANEL, :], NN, precision=HIGHEST, preferred_element_type=jnp.float32
        )
        xs[:, c : c + PANEL] = x
        if p > 0:
            aug[feats:, 0:c] = aug[feats:, 0:c] - lax.dot_general(
                x, aug[c : c + PANEL, 0:c], NN, precision=HIGHEST, preferred_element_type=jnp.float32
            )

    own = weights_ref.shape[1]
    mine = pl.ds(pl.multiple_of(lax.axis_index("feat") * own, PANEL), own)
    new_weights_ref[...] = weights_ref[...] + xs[0:classes, mine]
    x = split2(xs[...])
    frames = fh_ref.shape[1]

    for c in range(0, frames, WIDE):
        fitted = dot3(x, (fh_ref[:, c : c + WIDE], fl_ref[:, c : c + WIDE]), NN)
        new_residual_ref[:, c : c + WIDE] = residual_ref[:, c : c + WIDE] - fitted[:classes, :]


def per_device(inner, samples, residual, bank, bank_phase, bank_weights, block_index):
    chosen = block_index[0]
    local_projection = lax.dynamic_index_in_dim(bank, chosen, 0, keepdims=False)
    local_phases = lax.dynamic_index_in_dim(bank_phase, chosen, 0, keepdims=True)
    local_weights = lax.dynamic_index_in_dim(bank_weights, chosen, 0, keepdims=False)
    n_feat, n_rows = lax.axis_size("feat"), lax.axis_size("rows")
    depth, own = local_projection.shape
    feats = own * n_feat
    shard = jnp.concatenate([local_projection, jnp.pad(local_phases, ((0, round_up(depth + 1, 8) - depth - 1), (0, 0)))], axis=0)
    classes, frames = residual.shape
    total_rows = frames * n_feat * n_rows
    mine = jnp.where(lax.axis_index("rows") == 0, -ridge_weight * total_rows, 0.0) * local_weights
    extra = lax.dynamic_update_slice(
        jnp.zeros((classes, feats), jnp.float32), mine, (0, lax.axis_index("feat") * own)
    )
    tail = round_up(classes, 32)
    halves = own // PANEL
    peers = max(n_feat // 2 - 1, 1)
    packed_rows = round_up(panel_starts(feats, tail)[1], PIECES * n_feat * n_rows * 8)
    vmem = pl.BlockSpec(memory_space=pltpu.VMEM)
    params = pltpu.CompilerParams(vmem_limit_bytes=50 * 1024 * 1024)
    packed, fh, fl = pl.pallas_call(
        functools.partial(gram_kernel, depth),
        out_shape=(
            jax.ShapeDtypeStruct((packed_rows, PANEL), jnp.float32),
            jax.ShapeDtypeStruct((feats, frames), jnp.bfloat16),
            jax.ShapeDtypeStruct((feats, frames), jnp.bfloat16),
        ),
        in_specs=[vmem] * 4,
        out_specs=(vmem,) * 3,
        scratch_shapes=[
            pltpu.VMEM((n_feat, halves, shard.shape[0], PANEL), jnp.float32),
            pltpu.VMEM((depth, frames), jnp.bfloat16),
            pltpu.VMEM((depth, frames), jnp.bfloat16),
            pltpu.VMEM((tail, frames), jnp.bfloat16),
            pltpu.VMEM((tail, frames), jnp.bfloat16),
        ]
        + [pltpu.SemaphoreType.DMA((halves,))] * 2
        + [pltpu.SemaphoreType.DMA((peers, halves))] * 4,
        compiler_params=pltpu.CompilerParams(
            vmem_limit_bytes=50 * 1024 * 1024, collective_id=1, has_side_effects=True
        ),
        name="features_gram",
    )(shard, samples, residual, extra)
    packed = sum_everywhere(packed, sum_stages(n_feat, n_rows, inner))
    new_weights, new_residual = pl.pallas_call(
        functools.partial(solve_kernel, total_rows),
        out_shape=(
            jax.ShapeDtypeStruct(local_weights.shape, jnp.float32),
            jax.ShapeDtypeStruct(residual.shape, jnp.float32),
        ),
        in_specs=[vmem] * 5,
        out_specs=(vmem,) * 2,
        scratch_shapes=[
            pltpu.VMEM((feats + tail, feats), jnp.float32),
            pltpu.VMEM((feats, PANEL), jnp.float32),
            pltpu.VMEM((feats + tail, 6 * PANEL), jnp.bfloat16),
            pltpu.VMEM((feats, 6 * PANEL), jnp.bfloat16),
            pltpu.VMEM((tail, feats), jnp.float32),
        ],
        compiler_params=params,
        name="solve_fit",
    )(packed, fh, fl, residual, local_weights)
    return (new_weights, new_residual)


def near_size(devices):
    line = [getattr(d, "coords", None) for d in devices[0]]
    if any(c is None for c in line):
        return 2
    moved = [tuple(a != b for a, b in zip(c, line[0])) for c in line]
    for r in range(2, len(line)):
        if moved[r] != moved[1]:
            return r
    return len(line)


def solution(mesh):
    in_specs = (
        P(None, ("feat", "rows")),
        P(None, ("feat", "rows")),
        P(None, None, "feat"),
        P(None, "feat"),
        P(None, None, "feat"),
        P(),
    )
    out_specs = (P(None, "feat"), P(None, ("feat", "rows")))
    return jax.shard_map(
        functools.partial(per_device, near_size(mesh.devices)), mesh=mesh, in_specs=in_specs, out_specs=out_specs, check_vma=False
    )
```

```python
import functools
import math

import jax
import jax.numpy as jnp
from jax import lax
from jax.experimental import pallas as pl
from jax.experimental.pallas import tpu as pltpu
from jax.sharding import PartitionSpec as P

ridge_weight = 0.05
WIDE = 256
PANEL = 128
SUB = 8
SINE = (3.141592640144165, -5.167710084047848, 2.550077528428822, -0.598291299770303, 0.07765766117753167)
HIGHEST = lax.Precision.HIGHEST
NT = (((1,), (1,)), ((), ()))
NN = (((1,), (0,)), ((), ()))


def split2(x):
    hi = x.astype(jnp.bfloat16)
    lo = (x - hi.astype(jnp.float32)).astype(jnp.bfloat16)
    return hi, lo


def split3(x):
    hi = x.astype(jnp.bfloat16)
    rest = x - hi.astype(jnp.float32)
    mid = rest.astype(jnp.bfloat16)
    lo = (rest - mid.astype(jnp.float32)).astype(jnp.bfloat16)
    return hi, mid, lo


def dot3(a, b, dims):
    ah, al = a
    bh, bl = b
    f = functools.partial(lax.dot_general, dimension_numbers=dims, preferred_element_type=jnp.float32)
    return f(ah, bh) + (f(ah, bl) + f(al, bh))


def cosine(x):
    turns = x * (1.0 / (2.0 * math.pi))
    t = turns - jnp.round(turns)
    u = t * t
    s = SINE[-1]
    for c in SINE[-2::-1]:
        s = s * u + c
    s = s * t
    return 1.0 - 2.0 * (s * s)


def round_up(n, m):
    return -(-n // m) * m


def panel_starts(feats, tail):
    starts, at = [], 0
    for p in range(feats // PANEL):
        starts.append(at)
        at += feats - p * PANEL + tail
    return starts, at


def sum_stages(n_feat, n_rows, inner):
    return {
        "core": ("feat", 2, 1),
        "x": ("feat", n_feat // 2, 2),
        "near": ("rows", inner, 1),
        "far": ("rows", n_rows // inner, inner),
    }


ORDERS = (("core", "x", "near", "far"), ("core", "near", "x", "far"))


def slot_rows(rows, stages):
    sizes = []
    for order in ORDERS:
        n, line = rows, []
        for name in order:
            n //= stages[name][1]
            line.append(n)
        sizes.append(line)
    return sizes


def count_pieces(used, devices):
    least = round_up(used, 2 * devices * 8)
    return next(n for n in (8, 4, 2) if round_up(used, n * devices * 8) == least)


def sum_plan(stages, pieces, in_ref, out_ref, acc, scratch):
    depth = len(ORDERS[0])
    slots, recv_sems, send_sems = scratch[: 2 * depth], scratch[2 * depth : 4 * depth], scratch[4 * depth :]
    piece_rows = in_ref.shape[0] // pieces
    index = {"feat": lax.axis_index("feat"), "rows": lax.axis_index("rows")}
    place, peers = {}, {}
    for name, (axis, size, stride) in stages.items():
        here = lax.rem(lax.div(index[axis], stride), size)
        place[name] = here
        peers[name] = []
        for d in range(1, size):
            there = lax.rem(here + d, size)
            target = index[axis] + (there - here) * stride
            ids = (target, index["rows"]) if axis == "feat" else (index["feat"], target)
            peers[name].append((there, ids))

    def greet():
        barrier = pltpu.get_barrier_semaphore()
        count = 0
        for name in stages:
            for _, ids in peers[name]:
                pl.semaphore_signal(barrier, inc=1, device_id=ids, device_id_type=pl.DeviceIdType.MESH)
                count += 1
        pl.semaphore_wait(barrier, count)

    sends = []
    sizes = slot_rows(piece_rows, stages)
    bases = []
    for piece in range(pieces):
        base, line = piece * piece_rows, [piece * piece_rows]
        for level, name in enumerate(ORDERS[piece % 2]):
            base = base + place[name] * sizes[piece % 2][level]
            line.append(base)
        bases.append(line)

    def rows_at(start, n):
        return pl.ds(pl.multiple_of(start, 8), n)

    def start_reduce(piece, level):
        kind = piece % 2
        name, n = ORDERS[kind][level], sizes[kind][level]
        source = in_ref if level == 0 else acc
        copies = []
        for d, (there, ids) in enumerate(peers[name]):
            which = 2 * level + kind
            copy = pltpu.make_async_remote_copy(
                src_ref=source.at[rows_at(bases[piece][level] + there * n, n)],
                dst_ref=slots[which].at[piece // 2, d],
                send_sem=send_sems[which].at[0, piece // 2, d],
                recv_sem=recv_sems[which].at[0, piece // 2, d],
                device_id=ids,
                device_id_type=pl.DeviceIdType.MESH,
            )
            copy.start()
            copies.append(copy)
            sends.append(copy)
        return copies

    def end_reduce(piece, level, copies):
        kind = piece % 2
        n = sizes[kind][level]
        source = in_ref if level == 0 else acc
        target = out_ref if level == depth - 1 else acc
        mine = rows_at(bases[piece][level + 1], n)
        total = source[mine, :]
        for d, copy in enumerate(copies):
            copy.wait_recv()
            total = total + slots[2 * level + kind][piece // 2, d]
        target[mine, :] = total

    def start_gather(piece, level):
        kind = piece % 2
        name, n = ORDERS[kind][level], sizes[kind][level]
        mine = rows_at(bases[piece][level + 1], n)
        copies = []
        for d, (_, ids) in enumerate(peers[name]):
            which = 2 * level + kind
            copy = pltpu.make_async_remote_copy(
                src_ref=out_ref.at[mine],
                dst_ref=out_ref.at[mine],
                send_sem=send_sems[which].at[1, piece // 2, d],
                recv_sem=recv_sems[which].at[1, piece // 2, d],
                device_id=ids,
                device_id_type=pl.DeviceIdType.MESH,
            )
            copy.start()
            copies.append(copy)
            sends.append(copy)
        return copies

    def finish(flying):
        for level in range(depth):
            for piece in range(pieces):
                end_reduce(piece, level, flying[piece])
                if level + 1 < depth:
                    flying[piece] = start_reduce(piece, level + 1)
                else:
                    flying[piece] = start_gather(piece, level)
        for level in reversed(range(depth)):
            for piece in range(pieces):
                for copy in flying[piece]:
                    copy.wait_recv()
                if level > 0:
                    flying[piece] = start_gather(piece, level - 1)
        for copy in sends:
            copy.wait_send()

    return greet, start_reduce, finish


def sum_scratch(shape, pieces, stages):
    sizes = slot_rows(shape[0] // pieces, stages)
    slots, sems = [], []
    for level in range(len(ORDERS[0])):
        for kind in range(2):
            others = max(stages[ORDERS[kind][level]][1] - 1, 1)
            slots.append(pltpu.VMEM((pieces // 2, others, sizes[kind][level], shape[1]), jnp.float32))
            sems.append(pltpu.SemaphoreType.DMA((2, pieces // 2, others)))
    return [pltpu.VMEM(shape, jnp.float32)] * 2 + slots + sems + sems


def gram_kernel(
    depth, stages, pieces, own_ref, samples_ref, residual_ref, extra_ref, total_ref, fh_ref, fl_ref, bank, sh, sl, rh, rl, *sems
):
    core_send, core_recv, x_send, x_recv, pass_send, pass_recv, packed_ref, acc = sems[:8]
    greet, start_reduce, finish = sum_plan(stages, pieces, packed_ref, total_ref, acc, sems[8:])
    greet()
    feats = fh_ref.shape[0]
    classes = residual_ref.shape[0]
    tail = rh.shape[0]
    n_feat, halves = bank.shape[:2]
    n_x = n_feat // 2
    me, line = lax.axis_index("feat"), lax.axis_index("rows")
    core, x = lax.rem(me, 2), lax.div(me, 2)
    sibling = me + 1 - 2 * core
    after = [lax.rem(x + d, n_x) * 2 + core for d in range(1, n_x)]
    before = [lax.rem(x + n_x - d, n_x) * 2 + core for d in range(1, n_x)]

    def send(source, slot, half, send_sem, recv_sem, other):
        copy = pltpu.make_async_remote_copy(
            src_ref=source,
            dst_ref=bank.at[slot, half],
            send_sem=send_sem,
            recv_sem=recv_sem,
            device_id=(other, line),
            device_id_type=pl.DeviceIdType.MESH,
        )
        copy.start()
        return copy

    def own_half(half):
        return own_ref.at[:, half * PANEL : (half + 1) * PANEL]

    across, beside, passed = {}, {}, {}
    for half in range(halves):
        for d, other in enumerate(after):
            across[d, half] = send(own_half(half), me, half, x_send.at[d, half], x_recv.at[d, half], other)
    for half in range(halves):
        beside[half] = send(own_half(half), me, half, core_send.at[half], core_recv.at[half], sibling)

    starts, used = panel_starts(feats, tail)
    packed_ref[used:, :] = jnp.zeros_like(packed_ref[used:, :])
    h, l = split2(samples_ref[...])
    sh[...] = h
    sl[...] = l
    rh[...] = jnp.zeros_like(rh)
    rl[...] = jnp.zeros_like(rl)
    h, l = split2(residual_ref[...])
    rh[0:classes, :] = h
    rl[0:classes, :] = l

    def make_features(part, shard, half):
        turned = part.T
        inner = dot3(split2(turned[:, :depth]), (sh[...], sl[...]), NN)
        h, l = split2(cosine(inner + turned[:, depth : depth + 1]))
        rows = pl.ds(pl.multiple_of((shard * halves + half) * PANEL, PANEL), PANEL)
        fh_ref[rows, :] = h
        fl_ref[rows, :] = l

    for half in range(halves):
        make_features(own_ref[:, half * PANEL : (half + 1) * PANEL], me, half)
    for half in range(halves):
        beside[half].wait_recv()
        make_features(bank[sibling, half], sibling, half)
    for half in range(halves):
        for d, shard in enumerate(before):
            across[d, half].wait_recv()
            passed[d, half] = send(
                bank.at[shard, half], shard, half, pass_send.at[d, half], pass_recv.at[d, half], sibling
            )
            make_features(bank[shard, half], shard, half)
            passed[d, half].wait_recv()
            far = shard + 1 - 2 * core
            make_features(bank[far, half], far, half)
    for copies in (across, beside, passed):
        for copy in copies.values():
            copy.wait_send()

    flying = []
    for j in range(feats // WIDE):
        cols = slice(j * WIDE, (j + 1) * WIDE)
        even, odd = starts[2 * j], starts[2 * j + 1]
        other = (fh_ref[cols, :], fl_ref[cols, :])
        block = dot3(other, other, NT)
        packed_ref[even : even + WIDE, :] = block[:, :PANEL]
        packed_ref[odd : odd + PANEL, :] = block[PANEL:, PANEL:]

        @pl.loop(j + 1, feats // WIDE)
        def _(i):
            rows = pl.ds(pl.multiple_of(i * WIDE, WIDE), WIDE)
            below = (i - j) * WIDE
            block = dot3((fh_ref[rows, :], fl_ref[rows, :]), (fh_ref[cols, :], fl_ref[cols, :]), NT)
            packed_ref[pl.ds(pl.multiple_of(even + below, 32), WIDE), :] = block[:, :PANEL]
            packed_ref[pl.ds(pl.multiple_of(odd + below - PANEL, 32), WIDE), :] = block[:, PANEL:]

        right = dot3((rh[...], rl[...]), (fh_ref[cols, :], fl_ref[cols, :]), NT)
        for half, start in enumerate((even, odd)):
            c = j * WIDE + half * PANEL
            at = start + feats - c
            part = right[:, half * PANEL : (half + 1) * PANEL]
            packed_ref[at : at + tail, :] = part
            packed_ref[at : at + classes, :] = part[:classes, :] + extra_ref[:, c : c + PANEL]
        done = starts[2 * j + 2] if 2 * j + 2 < len(starts) else packed_ref.shape[0]
        while (len(flying) + 1) * (packed_ref.shape[0] // pieces) <= done and len(flying) < pieces:
            flying.append(start_reduce(len(flying), 0))
    finish(flying)


def spread_lane(x, lane):
    return jnp.broadcast_to(x[:, lane : lane + 1], x.shape)


def spread_row(x, row):
    return jnp.broadcast_to(x[row : row + 1, :], x.shape)


def inverse_factor(block):
    size = block.shape[0]
    shape = (SUB, size)
    row = lax.broadcasted_iota(jnp.int32, shape, 0)
    lane = lax.broadcasted_iota(jnp.int32, shape, 1)
    tiles = [block[t * SUB : (t + 1) * SUB, :] for t in range(size // SUB)]
    for s in range(size // SUB):
        base = s * SUB
        own = (lane >= base) & (lane < base + SUB)
        columns = [spread_lane(tiles[s], base + c) for c in range(SUB)]
        work = jnp.where(own, jnp.where(lane - base == row, 1.0, 0.0), tiles[s])
        pivots = []
        scale = jnp.zeros(shape, jnp.float32)
        for k in range(SUB):
            pivot_row = spread_row(work, k)
            heads = [spread_row(columns[c], k) for c in range(k, SUB)]
            inv = 1.0 / heads[0]
            scale = jnp.where(row == k, lax.rsqrt(heads[0]), scale)
            if k < SUB - 1:
                m = jnp.where(row > k, columns[k] * inv, 0.0)
                for c in range(k + 1, SUB):
                    columns[c] = columns[c] - m * heads[c - k]
                work = work - m * pivot_row
            pivots.append((inv, pivot_row, heads))
        tiles[s] = work * scale
        for t in range(s + 1, size // SUB):
            columns = [spread_lane(tiles[t], base + c) for c in range(SUB)]
            work = jnp.where(own, 0.0, tiles[t])
            for k, (inv, pivot_row, heads) in enumerate(pivots):
                m = columns[k] * inv
                for c in range(k + 1, SUB):
                    columns[c] = columns[c] - m * heads[c - k]
                work = work - m * pivot_row
            tiles[t] = work
    full = jnp.concatenate(tiles, axis=0)
    keep = lax.broadcasted_iota(jnp.int32, (size, size), 0) >= lax.broadcasted_iota(jnp.int32, (size, size), 1)
    return jnp.where(keep, full, 0.0)


def solve_kernel(total_rows, packed_ref, fh_ref, fl_ref, residual_ref, weights_ref, new_weights_ref, new_residual_ref, aug, linv, left, right, xs):
    feats = fh_ref.shape[0]
    classes = residual_ref.shape[0]
    height = aug.shape[0]
    tail = height - feats
    starts, _ = panel_starts(feats, tail)
    panels = feats // PANEL
    diag = lax.broadcasted_iota(jnp.int32, (PANEL, PANEL), 0) == lax.broadcasted_iota(jnp.int32, (PANEL, PANEL), 1)
    for p in range(panels):
        c = p * PANEL
        at = starts[p]
        aug[c : c + PANEL, c : c + PANEL] = packed_ref[at : at + PANEL, :] / total_rows + jnp.where(diag, ridge_weight, 0.0)
        aug[c + PANEL :, c : c + PANEL] = packed_ref[at + PANEL : at + height - c, :] / total_rows

    @pl.loop(0, panels)
    def _(p):
        at = pl.ds(pl.multiple_of(p * PANEL, PANEL), PANEL)
        inverse = inverse_factor(aug[at, at])
        linv[at, :] = inverse

        for q in range(panels):

            @pl.when(p == q)
            def _():
                c0 = (q + 1) * PANEL
                body = lax.dot_general(
                    aug[c0:, q * PANEL : c0], linv[q * PANEL : c0, :], NT, precision=HIGHEST, preferred_element_type=jnp.float32
                )
                aug[c0:, q * PANEL : c0] = body
                h, m, l = split3(body)
                for i, part in enumerate((h, h, m, h, l, m)):
                    left[c0:, i * PANEL : (i + 1) * PANEL] = part
                n = feats - c0
                if n > 0:
                    for i, part in enumerate((h, m, h, l, h, m)):
                        right[c0:feats, i * PANEL : (i + 1) * PANEL] = part[:n]
                c = c0
                while c < feats:
                    w = PANEL if c % WIDE else WIDE
                    aug[c:, c : c + w] = aug[c:, c : c + w] - lax.dot_general(
                        left[c:, :], right[c : c + w, :], NT, preferred_element_type=jnp.float32
                    )
                    c += w

    for p in reversed(range(panels)):
        c = p * PANEL
        x = lax.dot_general(
            aug[feats:, c : c + PANEL], linv[c : c + PANEL, :], NN, precision=HIGHEST, preferred_element_type=jnp.float32
        )
        xs[:, c : c + PANEL] = x
        if p > 0:
            aug[feats:, 0:c] = aug[feats:, 0:c] - lax.dot_general(
                x, aug[c : c + PANEL, 0:c], NN, precision=HIGHEST, preferred_element_type=jnp.float32
            )

    own = weights_ref.shape[1]
    mine = pl.ds(pl.multiple_of(lax.axis_index("feat") * own, PANEL), own)
    new_weights_ref[...] = weights_ref[...] + xs[0:classes, mine]
    x = split2(xs[...])
    frames = fh_ref.shape[1]

    for c in range(0, frames, WIDE):
        fitted = dot3(x, (fh_ref[:, c : c + WIDE], fl_ref[:, c : c + WIDE]), NN)
        new_residual_ref[:, c : c + WIDE] = residual_ref[:, c : c + WIDE] - fitted[:classes, :]


def per_device(inner, samples, residual, bank, bank_phase, bank_weights, block_index):
    chosen = block_index[0]
    local_projection = lax.dynamic_index_in_dim(bank, chosen, 0, keepdims=False)
    local_phases = lax.dynamic_index_in_dim(bank_phase, chosen, 0, keepdims=True)
    local_weights = lax.dynamic_index_in_dim(bank_weights, chosen, 0, keepdims=False)
    n_feat, n_rows = lax.axis_size("feat"), lax.axis_size("rows")
    depth, own = local_projection.shape
    feats = own * n_feat
    shard = jnp.concatenate([local_projection, jnp.pad(local_phases, ((0, round_up(depth + 1, 8) - depth - 1), (0, 0)))], axis=0)
    classes, frames = residual.shape
    total_rows = frames * n_feat * n_rows
    mine = jnp.where(lax.axis_index("rows") == 0, -ridge_weight * total_rows, 0.0) * local_weights
    extra = lax.dynamic_update_slice(
        jnp.zeros((classes, feats), jnp.float32), mine, (0, lax.axis_index("feat") * own)
    )
    tail = round_up(classes, 32)
    halves = own // PANEL
    peers = max(n_feat // 2 - 1, 1)
    used = panel_starts(feats, tail)[1]
    stages, pieces = sum_stages(n_feat, n_rows, inner), count_pieces(used, n_feat * n_rows)
    packed_rows = round_up(used, pieces * n_feat * n_rows * 8)
    vmem = pl.BlockSpec(memory_space=pltpu.VMEM)
    params = pltpu.CompilerParams(vmem_limit_bytes=50 * 1024 * 1024)
    packed, fh, fl = pl.pallas_call(
        functools.partial(gram_kernel, depth, stages, pieces),
        out_shape=(
            jax.ShapeDtypeStruct((packed_rows, PANEL), jnp.float32),
            jax.ShapeDtypeStruct((feats, frames), jnp.bfloat16),
            jax.ShapeDtypeStruct((feats, frames), jnp.bfloat16),
        ),
        in_specs=[vmem] * 4,
        out_specs=(vmem,) * 3,
        scratch_shapes=[
            pltpu.VMEM((n_feat, halves, shard.shape[0], PANEL), jnp.float32),
            pltpu.VMEM((depth, frames), jnp.bfloat16),
            pltpu.VMEM((depth, frames), jnp.bfloat16),
            pltpu.VMEM((tail, frames), jnp.bfloat16),
            pltpu.VMEM((tail, frames), jnp.bfloat16),
        ]
        + [pltpu.SemaphoreType.DMA((halves,))] * 2
        + [pltpu.SemaphoreType.DMA((peers, halves))] * 4
        + sum_scratch((packed_rows, PANEL), pieces, stages),
        compiler_params=pltpu.CompilerParams(
            vmem_limit_bytes=50 * 1024 * 1024, collective_id=0, has_side_effects=True
        ),
        name="features_sum",
    )(shard, samples, residual, extra)
    new_weights, new_residual = pl.pallas_call(
        functools.partial(solve_kernel, total_rows),
        out_shape=(
            jax.ShapeDtypeStruct(local_weights.shape, jnp.float32),
            jax.ShapeDtypeStruct(residual.shape, jnp.float32),
        ),
        in_specs=[vmem] * 5,
        out_specs=(vmem,) * 2,
        scratch_shapes=[
            pltpu.VMEM((feats + tail, feats), jnp.float32),
            pltpu.VMEM((feats, PANEL), jnp.float32),
            pltpu.VMEM((feats + tail, 6 * PANEL), jnp.bfloat16),
            pltpu.VMEM((feats, 6 * PANEL), jnp.bfloat16),
            pltpu.VMEM((tail, feats), jnp.float32),
        ],
        compiler_params=params,
        name="solve_fit",
    )(packed, fh, fl, residual, local_weights)
    return (new_weights, new_residual)


def near_size(devices):
    line = [getattr(d, "coords", None) for d in devices[0]]
    if any(c is None for c in line):
        return 2
    moved = [tuple(a != b for a, b in zip(c, line[0])) for c in line]
    for r in range(2, len(line)):
        if moved[r] != moved[1]:
            return r
    return len(line)


def solution(mesh):
    in_specs = (
        P(None, ("feat", "rows")),
        P(None, ("feat", "rows")),
        P(None, None, "feat"),
        P(None, "feat"),
        P(None, None, "feat"),
        P(),
    )
    out_specs = (P(None, "feat"), P(None, ("feat", "rows")))
    return jax.shard_map(
        functools.partial(per_device, near_size(mesh.devices)), mesh=mesh, in_specs=in_specs, out_specs=out_specs, check_vma=False
    )
```
